128 devices in a mesh: fsdp: 128 (over y, z, x, core).
Axes of the slice: x: 4, y: 4, z: 4, core: 2. Of those that a mesh axis runs over, the one named last changes fastest.
Arguments:
- tokens: bfloat16 [16384, 896], P('fsdp'), may hold values from -6 to 6
- cotangent: bfloat16 [16384, 896], P('fsdp'), may hold values from -6 to 6
- lengths: int32 [6], replicated, may hold values from 1 to 8192, 16384 in all
- in_weight: float32 [896, 1152], P('fsdp'), may hold values from -0.1875 to 0.1875
- out_weight: float32 [896, 896], P(None, 'fsdp'), may hold values from -2.5 to 2.5
- gate_weight: float32 [896, 9728], P('fsdp'), may hold values from -0.1875 to 0.1875
- down_weight: float32 [4864, 896], P('fsdp'), may hold values from -0.078125 to 0.078125
- gains: float32 [2, 896], P(None, 'fsdp'), may hold values from 0.8 to 2.7
- in_first: float32 [896, 1152], P('fsdp'), may hold values from -0.000397325 to 0.000397325
- out_first: float32 [896, 896], P(None, 'fsdp'), may hold values from -1.8996278e-05 to 1.8996278e-05
- gate_first: float32 [896, 9728], P('fsdp'), may hold values from -4.98599e-05 to 4.98599e-05
- down_first: float32 [4864, 896], P('fsdp'), may hold values from -0.00012207072 to 0.00012207072
- gains_first: float32 [2, 896], P(None, 'fsdp'), may hold values from -0.00028977904 to 0.00028977904
- in_second: float32 [896, 1152], P('fsdp'), may hold values from 1.6607624e-08 to 6.63042e-08
- out_second: float32 [896, 896], P(None, 'fsdp'), may hold values from 3.7962317e-11 to 1.5156058e-10
- gate_second: float32 [896, 9728], P('fsdp'), may hold values from 2.6152822e-10 to 1.0441241e-09
- down_second: float32 [4864, 896], P('fsdp'), may hold values from 1.5676126e-09 to 6.2585297e-09
- gains_second: float32 [2, 896], P(None, 'fsdp'), may hold values from 8.833842e-09 to 3.526819e-08
Outputs:
- output: bfloat16 [16384, 896], P('fsdp')
- input_grad: bfloat16 [16384, 896], P('fsdp')
- in_master: float32 [896, 1152], P('fsdp')
- in_moment: float32 [896, 1152], P('fsdp')
- in_square: float32 [896, 1152], P('fsdp')
- in_copy: bfloat16 [896, 1152], P('fsdp')
- out_master: float32 [896, 896], P(None, 'fsdp')
- out_moment: float32 [896, 896], P(None, 'fsdp')
- out_square: float32 [896, 896], P(None, 'fsdp')
- out_copy: bfloat16 [896, 896], P(None, 'fsdp')
- gate_master: float32 [896, 9728], P('fsdp')
- gate_moment: float32 [896, 9728], P('fsdp')
- gate_square: float32 [896, 9728], P('fsdp')
- gate_copy: bfloat16 [896, 9728], P('fsdp')
- down_master: float32 [4864, 896], P('fsdp')
- down_moment: float32 [4864, 896], P('fsdp')
- down_square: float32 [4864, 896], P('fsdp')
- down_copy: bfloat16 [4864, 896], P('fsdp')
- gains_master: float32 [2, 896], P(None, 'fsdp')
- gains_moment: float32 [2, 896], P(None, 'fsdp')
- gains_square: float32 [2, 896], P(None, 'fsdp')
- gains_copy: bfloat16 [2, 896], P(None, 'fsdp')
- grad_norm: float32 [], replicated
The draws below stay inside these ranges and needn't reach their ends.
Inputs may be any that keep to these rules, and one draw needn't show every extreme that they name: The 6 lengths sum to 16384, and the longest is exactly 8192.
All inputs are finite; a program needn't handle non-finite values.
Results may differ from the reference program's by a relative error of at most 0.019.
The reference program's roundings to bfloat16 on the way count: a program that leaves them out, or rounds other values in their place, can miss the bound.
Values may be sent and summed in bfloat16 or wider, within the bound.
A program may use at most 320 MiB of HBM per device.

```python
import math
import jax
import jax.numpy as jnp
import numpy as np
from jax import lax

D = 896
FF = 4864
HEADS = 14
KV_HEADS = 2
HEAD_DIM = 64
STEP = 10
TOKENS = 16384
MAXDOC = 8192
DOCS = 6
QW = 896
QKVW = 1152
OUT_FAN = 5


def draw_gains(key, part):
    key = jax.random.fold_in(key, 7)
    incline = 0.73
    along_width = jnp.arange(D, dtype=jnp.float32) / max(D - 1, 1)
    jitter = jax.random.uniform(key, (2, D), jnp.float32, 0.8, 1.2)
    return (1.0 + incline * along_width)[None, :] * jitter


def block_scale(stream_key, shape, shards, smallest, high):
    loudness, own = 1.0, jax.random.fold_in(stream_key, 6)
    for axis_at, blocks in shards:
        heights = jnp.exp(jax.random.uniform(jax.random.fold_in(own, axis_at), (blocks,), jnp.float32, smallest / len(shards), high / len(shards)))
        loudness = loudness * jnp.repeat(heights, shape[axis_at] // blocks).reshape([-1 if axis == axis_at else 1 for axis in range(len(shape))])
    return loudness


def split_up(count, total, reach, lean):
    weights = [(1 << 20) // math.isqrt(rank ** lean) + 1 for rank in range(2, count + 1)]
    rest, counts = total - reach - (count - 1), [1] * (count - 1)
    while rest > 0:
        movable = [i for i in range(count - 1) if counts[i] < reach]
        mass, budget = sum([weights[i] for i in movable]), rest
        for i in movable:
            addition = min(reach - counts[i], max(1, budget * weights[i] // mass), rest)
            counts[i] = counts[i] + addition
            rest = rest - addition
    return np.array([reach] + counts)


def uneven(rng, amount, total, limit, lean):
    if amount == 2:
        one = jax.random.randint(rng, (), max(1, total - limit), min(limit, total - 1) + 1)
        return jnp.stack([one, total - one])
    sizes = jnp.asarray(split_up(amount, total, limit, lean), jnp.int32)
    pairs = (amount - 1) // 2
    giver, receiver = sizes[1:1 + 2 * pairs:2], sizes[2:2 + 2 * pairs:2]
    slack = jnp.minimum(giver - 1, limit - receiver)
    moved = jax.random.randint(jax.random.fold_in(rng, 1), (pairs,), 0, 1 << 20) % (slack + 1)
    sizes = sizes.at[1:1 + 2 * pairs:2].set(giver - moved).at[2:2 + 2 * pairs:2].set(receiver + moved)
    return sizes[jax.random.permutation(jax.random.fold_in(rng, 2), amount)]


def gaussian(rng, dims, spread, limit, cuts=(), kind=jnp.bfloat16):
    entries = spread * jax.random.normal(rng, dims, jnp.float32)
    if cuts:
        entries = entries * block_scale(rng, dims, cuts, -0.22, 0.18)
    return jnp.clip(entries, -limit, limit).astype(kind)


def setup_inputs(seed: int = 0) -> dict:
    seeds = jax.random.split(jax.random.key(seed), 19)
    tokens = gaussian(seeds[0], (TOKENS, D), 1.0, 6.0, ((0, 128),))
    cotangent = gaussian(seeds[1], (TOKENS, D), 1.0, 6.0, ((0, 128),))
    lengths = uneven(seeds[2], DOCS, TOKENS, MAXDOC, 1).astype(jnp.int32)
    in_weight = gaussian(seeds[3], (D, QKVW), D ** -0.5, 0.1875, ((0, 128),), jnp.float32)
    out_weight = gaussian(seeds[4], (QW, D), OUT_FAN ** -0.5, 2.5, ((1, 128),), jnp.float32)
    gate_weight = gaussian(seeds[5], (D, 2 * FF), D ** -0.5, 0.1875, ((0, 128),), jnp.float32)
    down_weight = gaussian(seeds[6], (FF, D), FF ** -0.5, 0.078125, ((0, 128),), jnp.float32)
    gains = draw_gains(jax.random.fold_in(seeds[18], 71), 0)
    in_first = gaussian(seeds[8], (D, QKVW), (0.111 * (0.094 / (OUT_FAN * (0.094 * QKVW * D / OUT_FAN + 6.9 * OUT_FAN + 2.88 * D + 1.59 * FF + 0.1 * D / OUT_FAN))) ** 0.5), 0.000397325, ((0, 128),), jnp.float32)
    out_first = gaussian(seeds[9], (QW, D), (0.111 * (6.9 * OUT_FAN / (QW * D * (0.094 * QKVW * D / OUT_FAN + 6.9 * OUT_FAN + 2.88 * D + 1.59 * FF + 0.1 * D / OUT_FAN))) ** 0.5), 1.8996277503902093e-05, ((1, 128),), jnp.float32)
    gate_first = gaussian(seeds[10], (D, 2 * FF), (0.111 * (1.44 / (FF * (0.094 * QKVW * D / OUT_FAN + 6.9 * OUT_FAN + 2.88 * D + 1.59 * FF + 0.1 * D / OUT_FAN))) ** 0.5), 4.9859900173032656e-05, ((0, 128),), jnp.float32)
    down_first = gaussian(seeds[11], (FF, D), (0.111 * (1.59 / (D * (0.094 * QKVW * D / OUT_FAN + 6.9 * OUT_FAN + 2.88 * D + 1.59 * FF + 0.1 * D / OUT_FAN))) ** 0.5), 0.00012207072, ((0, 128),), jnp.float32)
    gains_first = gaussian(seeds[12], (2, D), (0.111 * (0.05 / (OUT_FAN * (0.094 * QKVW * D / OUT_FAN + 6.9 * OUT_FAN + 2.88 * D + 1.59 * FF + 0.1 * D / OUT_FAN))) ** 0.5), 0.00028977904, ((1, 128),), jnp.float32)
    in_second = jnp.clip(jnp.exp(math.log(6.63042030168981e-08) - 1.3843914 * jax.random.uniform(seeds[13], (D, QKVW), jnp.float32) ** block_scale(seeds[13], (D, QKVW), ((0, 128),), -0.2, 0.2)), 1.6607623720688025e-08, 6.63042030168981e-08)
    out_second = jnp.clip(jnp.exp(math.log(1.515605835278322e-10) - 1.3843914 * jax.random.uniform(seeds[14], (QW, D), jnp.float32) ** block_scale(seeds[14], (QW, D), ((1, 128),), -0.2, 0.2)), 3.796231731745259e-11, 1.515605835278322e-10)
    gate_second = jnp.clip(jnp.exp(math.log(1.0441241204972584e-09) - 1.38439147 * jax.random.uniform(seeds[15], (D, 2 * FF), jnp.float32) ** block_scale(seeds[15], (D, 2 * FF), ((0, 128),), -0.2, 0.2)), 2.6152821575031737e-10, 1.0441241204972584e-09)
    down_second = jnp.clip(jnp.exp(math.log(6.258529694491699e-09) - 1.38439146 * jax.random.uniform(seeds[16], (FF, D), jnp.float32) ** block_scale(seeds[16], (FF, D), ((0, 128),), -0.2, 0.2)), 1.567612595287926e-09, 6.258529694491699e-09)
    gains_second = jnp.clip(jnp.exp(math.log(3.526819014609828e-08) - 1.3843914 * jax.random.uniform(seeds[17], (2, D), jnp.float32) ** block_scale(seeds[17], (2, D), ((1, 128),), -0.2, 0.2)), 8.833842102262679e-09, 3.526819014609828e-08)
    return {"tokens": tokens, "cotangent": cotangent, "lengths": lengths, "in_weight": in_weight, "out_weight": out_weight, "gate_weight": gate_weight, "down_weight": down_weight, "gains": gains, "in_first": in_first, "out_first": out_first, "gate_first": gate_first, "down_first": down_first, "gains_first": gains_first, "in_second": in_second, "out_second": out_second, "gate_second": gate_second, "down_second": down_second, "gains_second": gains_second}


@jax.custom_vjp
def low(v):
    return lax.optimization_barrier(v.astype(jnp.bfloat16)).astype(jnp.float32)

@jax.custom_vjp
def low_back(v):
    return v

def low_keep(v):
    return (low(v), None)

def low_pass(kept, grad):
    return (grad,)

def back_keep(v):
    return (v, None)

def back_low(kept, grad):
    return (low(grad),)
low.defvjp(low_keep, low_pass)
low_back.defvjp(back_keep, back_low)
norm_eps = 1e-05
rope_base = 130000.0
beta_first = 0.9
beta_second = 0.95
adam_eps = 1e-08
decay_rate = 0.1
matrix_rate = 4.0
gain_rate = 1.5
masked_score = -1e+30
highest = lax.Precision.HIGHEST

def product(left_side, right_side):
    return jnp.dot(left_side, right_side, precision=highest, preferred_element_type=jnp.float32)

def rms_norm(values, gain_row):
    scale_rows = lax.rsqrt(lax.optimization_barrier(jnp.mean(values * values, axis=-1, keepdims=True)) + norm_eps)
    return values * scale_rows * gain_row

def rotate(values, cosine, sine):
    middle = values.shape[-1] // 2
    turned = jnp.concatenate([-values[..., middle:], values[..., :middle]], axis=-1)
    return values * cosine + turned * sine

def locate(position, lengths):
    doc_ends = jnp.cumsum(lengths).astype(jnp.int32)
    starts = (doc_ends - lengths).astype(jnp.int32)
    inside = (position[:, None] >= starts[None, :]) & (position[:, None] < doc_ends[None, :])
    number = jnp.arange(lengths.shape[0], dtype=jnp.int32)
    document = lax.optimization_barrier(jnp.sum(jnp.where(inside, number[None, :], 0), axis=1)).astype(jnp.int32)
    offset = lax.optimization_barrier(jnp.sum(jnp.where(inside, starts[None, :], 0), axis=1)).astype(jnp.int32)
    return (document, (position - offset).astype(jnp.int32))

def rotation_table(doc_place):
    half_dim = HEAD_DIM // 2
    inverse = rope_base ** (-(jnp.arange(half_dim, dtype=jnp.float32) * 2.0) / HEAD_DIM)
    angles = doc_place.astype(jnp.float32)[:, None] * inverse[None, :]
    angles = jnp.concatenate([angles, angles], axis=1)
    return (jnp.cos(angles)[:, None, :], jnp.sin(angles)[:, None, :])

def attend(queries, key_rows, value_rows, document):
    height = min(512, TOKENS)
    window = min(TOKENS, MAXDOC + height)
    group_size = HEADS // KV_HEADS
    score_scale = HEAD_DIM ** (-0.5)

    def one_block(number):
        first_row = number * height
        key_begin = jnp.clip(first_row + height - window, 0, TOKENS - window)
        block_query = lax.dynamic_slice_in_dim(queries, first_row, height, 0).reshape(height, KV_HEADS, group_size, HEAD_DIM)
        key_window = lax.dynamic_slice_in_dim(key_rows, key_begin, window, 0)
        value_window = lax.dynamic_slice_in_dim(value_rows, key_begin, window, 0)
        query_doc = lax.dynamic_slice_in_dim(document, first_row, height, 0)
        key_doc = lax.dynamic_slice_in_dim(document, key_begin, window, 0)
        query_pos = first_row + jnp.arange(height, dtype=jnp.int32)
        key_pos = key_begin + jnp.arange(window, dtype=jnp.int32)
        allowed = (query_doc[:, None] == key_doc[None, :]) & (key_pos[None, :] <= query_pos[:, None])
        raw_scores = low_back(jnp.einsum('qkgd,skd->kgqs', block_query, key_window, precision=highest))
        scores = jnp.where(allowed[None, None], raw_scores * score_scale, masked_score)
        highest_score = lax.optimization_barrier(jnp.max(scores, axis=-1, keepdims=True))
        log_total = highest_score + jnp.log(lax.optimization_barrier(jnp.sum(jnp.exp(scores - highest_score), axis=-1, keepdims=True)))
        weights = jnp.exp(scores - log_total)
        mixed = jnp.einsum('kgqs,skd->qkgd', low(weights), value_window, precision=highest)
        return mixed.reshape(height, HEADS * HEAD_DIM)
    pieces = lax.map(jax.checkpoint(one_block), jnp.arange(TOKENS // height, dtype=jnp.int32))
    return pieces.reshape(TOKENS, HEADS * HEAD_DIM)

def forward(inputs, in_weight, out_weight, gate_weight, down_weight, gains, document, cosine, sine):
    query_width = HEADS * HEAD_DIM
    key_width = KV_HEADS * HEAD_DIM
    gain_rows = low(gains)
    normed = low(rms_norm(inputs, gain_rows[0]))
    joined = low_back(product(normed, low(in_weight)))
    queries = joined[:, :query_width].reshape(TOKENS, HEADS, HEAD_DIM)
    key_rows = joined[:, query_width:query_width + key_width].reshape(TOKENS, KV_HEADS, HEAD_DIM)
    value_rows = joined[:, query_width + key_width:].reshape(TOKENS, KV_HEADS, HEAD_DIM)
    queries = low(rotate(queries, cosine, sine))
    key_rows = low(rotate(key_rows, cosine, sine))
    value_rows = low(value_rows)
    mixed = low_back(low(attend(queries, key_rows, value_rows, document)))
    middle = inputs + low_back(product(mixed, low(out_weight)))
    normed_two = low(rms_norm(middle, gain_rows[1]))
    gate_both = low_back(product(normed_two, low(gate_weight)))
    gate_part = gate_both[:, :FF]
    hidden = low(gate_part / (1.0 + jnp.exp(-gate_part)) * gate_both[:, FF:])
    return middle + product(hidden, low(down_weight))

def adam_step(weight, gradient, moment, square, factor, step_rate):
    gradient = gradient * factor
    moment = beta_first * moment + (1.0 - beta_first) * gradient
    square = beta_second * square + (1.0 - beta_second) * gradient * gradient
    moment_hat = moment / (1.0 - beta_first ** STEP)
    square_hat = square / (1.0 - beta_second ** STEP)
    updated = weight - step_rate * (moment_hat / (jnp.sqrt(square_hat) + adam_eps) + decay_rate * weight)
    return (updated, moment, square, updated.astype(jnp.bfloat16))

def reference(tokens, cotangent, lengths, in_weight, out_weight, gate_weight, down_weight, gains, in_first, out_first, gate_first, down_first, gains_first, in_second, out_second, gate_second, down_second, gains_second):
    position = jnp.arange(TOKENS, dtype=jnp.int32)
    document, doc_place = locate(position, lengths)
    cosine, sine = rotation_table(doc_place)
    inputs = tokens.astype(jnp.float32)

    def apply_layer(layer_in, w_in, w_out, w_gate, w_down, w_gains):
        return forward(layer_in, w_in, w_out, w_gate, w_down, w_gains, document, cosine, sine)
    output, pullback = jax.vjp(apply_layer, inputs, in_weight, out_weight, gate_weight, down_weight, gains)
    gradients = pullback(cotangent.astype(jnp.float32))
    squares = sum((jnp.sum(gradient * gradient) for gradient in gradients[1:]))
    grad_norm = jnp.sqrt(squares)
    factor = 1.0 / jnp.maximum(grad_norm, 1.0)
    in_new = adam_step(in_weight, gradients[1], in_first, in_second, factor, matrix_rate * D ** (-0.5))
    out_new = adam_step(out_weight, gradients[2], out_first, out_second, factor, matrix_rate * OUT_FAN ** (-0.5))
    gate_new = adam_step(gate_weight, gradients[3], gate_first, gate_second, factor, matrix_rate * D ** (-0.5))
    down_new = adam_step(down_weight, gradients[4], down_first, down_second, factor, matrix_rate * FF ** (-0.5))
    gains_new = adam_step(gains, gradients[5], gains_first, gains_second, factor, gain_rate)
    return (output.astype(jnp.bfloat16), gradients[0].astype(jnp.bfloat16), in_new[0], in_new[1], in_new[2], in_new[3], out_new[0], out_new[1], out_new[2], out_new[3], gate_new[0], gate_new[1], gate_new[2], gate_new[3], down_new[0], down_new[1], down_new[2], down_new[3], gains_new[0], gains_new[1], gains_new[2], gains_new[3], grad_norm)
```

```python
import jax
import jax.numpy as jnp
import numpy as np
from jax import lax
from jax.experimental import pallas as pl
from jax.experimental.pallas import tpu as pltpu
from jax.sharding import Mesh
from jax.sharding import PartitionSpec as P

D = 896
FF = 4864
HEADS = 14
KV_HEADS = 2
HEAD_DIM = 64
DOCS = 6
STEP = 10

norm_eps = 1e-05
rope_base = 130000.0
beta_first = 0.9
beta_second = 0.95
adam_eps = 1e-08
decay_rate = 0.1
matrix_rate = 4.0
gain_rate = 1.5
masked_score = -1e30

ALL = ("y", "z", "x", "c")
RING = 4
DEVICES = 128
CHIPS = 64
LOCAL = 128
CHIP = 2 * LOCAL
GROUP = HEADS // KV_HEADS
HALF_Q = GROUP * HEAD_DIM
RANKS = 8
SLICE = FF // RANKS
DOWN_ROWS = FF // DEVICES
DOWN_PAD = 48
SPAN = 16
BLOCKS = LOCAL // SPAN
TILE = SPAN * DEVICES
HALF = SPAN // 2
HALF_TILE = TILE // 2
HALF_ROWS = GROUP * SPAN
QROWS = 2 * HALF_ROWS
QPAD = 256
WIDE = 8 * DEVICES
IN_COLS, OUT_COLS = 640, 512
ATT_COLS = IN_COLS + OUT_COLS
HEADS_6 = 6 * HEAD_DIM
LATE = 2 * HEADS_6
LAST = LATE + 256
GAIN_AT = LAST + HEAD_DIM
HID = 640
MESH = pl.DeviceIdType.MESH
VM, ANY = pltpu.VMEM, pl.ANY
bf16 = jnp.bfloat16
f32 = jnp.float32


def widen_matrix(turned=False):
    place = np.arange(WIDE)
    picks = np.zeros((D, WIDE), np.float32)
    kept = place % 8 < 7
    picks[(7 * (place // 8) + place % 8)[kept], place[kept]] = 1
    return jnp.asarray(picks.T if turned else picks, bf16)


def pack_matrix():
    unit = np.arange(SLICE)
    picks = np.zeros((HID, 16 * DOWN_PAD), np.float32)
    picks[unit, DOWN_PAD * (unit // DOWN_ROWS) + unit % DOWN_ROWS] = 1
    return jnp.asarray(picks, bf16)


def turn_matrix():
    place = np.arange(DEVICES)
    picks = np.zeros((DEVICES, DEVICES), np.float32)
    picks[place % RANKS * 16 + place // RANKS, place] = 1
    return jnp.asarray(picks, bf16)


def order_matrix():
    place = np.arange(CHIP)
    picks = np.zeros((CHIP, CHIP), np.float32)
    picks[(place % LOCAL // 8 * 2 + place // LOCAL) * 8 + place % 8, place] = 1
    return jnp.asarray(picks, bf16)


def swap_matrix():
    place = np.arange(DEVICES)
    picks = np.zeros((DEVICES, DEVICES), np.float32)
    picks[place // 8 % RING * 32 + place // 32 * 8 + place % 8, place] = 1
    return jnp.asarray(picks, bf16)


def step_along(axis, delta):
    size = 2 if axis == "c" else RING
    return {axis: lax.rem(lax.axis_index(axis) + (delta + size), size)}


def shifted(axis, delta):
    return lax.rem(lax.axis_index(axis) + (delta + RING), RING)


def axis_peers(axes):
    peers = []
    for axis in axes:
        peers += [step_along(axis, delta) for delta in ((1,) if axis == "c" else (1, 2, 3))]
    return peers


def line_peers():
    x, c = lax.axis_index("x"), lax.axis_index("c")
    return [
        {"x": lax.rem(x + dx, RING), "c": lax.rem(c + dc, 2)}
        for dx in range(RING)
        for dc in range(2)
        if dx or dc
    ]


def device_number():
    y, z, x, c = (lax.axis_index(axis) for axis in ALL)
    return ((y * RING + z) * RING + x) * 2 + c


def place(index):
    return {
        "y": index // 32,
        "z": lax.rem(index // 8, 4),
        "x": lax.rem(index // 2, 4),
        "c": lax.rem(index, 2),
    }


def greet(peers, target=None, source=None):
    barrier = pltpu.get_barrier_semaphore()
    for peer in peers:
        pl.semaphore_signal(barrier, inc=1, device_id=peer, device_id_type=MESH)
    if target is None:
        pl.semaphore_wait(barrier, len(peers))
        return
    me = device_number()

    @pl.when(target != me)
    def _():
        pl.semaphore_signal(barrier, inc=1, device_id=place(source), device_id_type=MESH)
        pl.semaphore_wait(barrier, len(peers) + 1)

    @pl.when(target == me)
    def _():
        pl.semaphore_wait(barrier, len(peers))


class Sems:
    def __init__(self, send, recv):
        self.send, self.recv, self.used = send, recv, 0

    def copy(self, src, dst, device):
        at = self.used
        self.used += 1
        return pltpu.make_async_remote_copy(
            src_ref=src,
            dst_ref=dst,
            send_sem=self.send.at[at],
            recv_sem=self.recv.at[at],
            device_id=device,
            device_id_type=MESH,
        )

    def local(self, src, dst):
        at = self.used
        self.used += 1
        return pltpu.make_async_copy(src, dst, self.send.at[at])

    def fetch(self, src, dst):
        copy = self.local(src, dst)
        copy.start()
        return copy


def together(*steps):
    running = list(steps)
    while running:
        for step in list(running):
            try:
                next(step)
            except StopIteration:
                running.remove(step)


def gather_direct(sems, axis, part):
    me = shifted(axis, 0)
    copies = [sems.copy(part(me), part(me), step_along(axis, d)) for d in (1, 3, 2)]
    for copy in copies:
        copy.start()
    yield
    for copy in copies:
        copy.wait()


def gather_ring(sems, axis, part, half):
    me, left, right = shifted(axis, 0), shifted(axis, -1), shifted(axis, 1)
    to_right = sems.copy(part(me), part(me), step_along(axis, 1))
    to_left = sems.copy(part(me), part(me), step_along(axis, -1))
    to_right.start()
    to_left.start()
    yield
    to_right.wait_recv()
    on_right = sems.copy(half(left, 0), half(left, 0), step_along(axis, 1))
    on_right.start()
    to_left.wait_recv()
    on_left = sems.copy(half(right, 1), half(right, 1), step_along(axis, -1))
    on_left.start()
    yield
    on_right.wait_recv()
    on_left.wait_recv()
    for copy in (to_right, to_left, on_right, on_left):
        copy.wait_send()


def chip_gather(sems, order, buf):
    for number, axis in enumerate(order):
        own = tuple(lax.axis_index(a) for a in reversed(order[number + 1 :]))

        def part(i, own=own):
            return buf.at[(*own, i)]

        if number < len(order) - 1:
            yield from gather_direct(sems, axis, part)
        else:
            yield from gather_ring(sems, axis, part, lambda i, h: buf.at[i, pl.ds(2 * h, 2)])


def own_place(axes):
    return tuple(lax.axis_index(axis) for axis in axes)


def natural(axes):
    return [
        tuple({"y": y, "z": z, "x": x}[axis] for axis in axes)
        for y in range(RING)
        for z in range(RING)
        for x in range(RING)
    ]


def in_turn(phases):
    for phase in phases:
        phase()
        yield


def gather_line(sems, all_ref):
    x, c = lax.axis_index("x"), lax.axis_index("c")
    sibling, right, left = step_along("c", 1), step_along("x", 1), step_along("x", -1)
    at_left, at_right, at_far = shifted("x", -1), shifted("x", 1), shifted("x", 2)
    top, bottom = pl.ds(0, LOCAL // 2), pl.ds(LOCAL // 2, LOCAL // 2)

    def same(ref, device):
        return sems.copy(ref, ref, device)

    mine = all_ref.at[x, c]
    to_right, to_left, to_pair = same(mine, right), same(mine, left), same(mine, sibling)
    on_right = same(all_ref.at[at_left, c, top], right)
    on_left = same(all_ref.at[at_right, c, bottom], left)
    pair_left = same(all_ref.at[at_left, c], sibling)
    pair_right = same(all_ref.at[at_right, c], sibling)
    pair_far = same(all_ref.at[at_far, c], sibling)

    def start():
        to_right.start()
        to_left.start()
        to_pair.start()

    def relay():
        to_right.wait_recv()
        on_right.start()
        pair_left.start()
        to_left.wait_recv()
        on_left.start()
        pair_right.start()
        pair_left.wait_recv()

    def relay_far():
        on_right.wait_recv()
        on_left.wait_recv()
        pair_far.start()

    def close():
        for copy in (to_right, to_left, to_pair, on_right, on_left, pair_left, pair_right, pair_far):
            copy.wait_send()

    return start, to_pair.wait_recv, relay, pair_right.wait_recv, relay_far, pair_far.wait_recv, close


def add_into(out, *terms):
    total = terms[0][...].astype(f32)
    for term in terms[1:]:
        total = total + term[...].astype(f32)
    out[...] = total.astype(out.dtype)


def half_of(ref, h):
    return ref.at[pl.ds(2 * h, 2)]


def reduce_ring(sems, axis, part, bufs, out):
    first, next_right, next_left, last_left, last_right = bufs
    me, left, right, far = (shifted(axis, d) for d in (0, -1, 1, 2))
    one = sems.copy(half_of(part(far), 0), half_of(first, 0), step_along(axis, 1))
    two = sems.copy(half_of(part(far), 1), half_of(first, 1), step_along(axis, -1))
    one.start()
    two.start()
    half_of(next_right, 1)[...] = half_of(part(right), 1)[...]
    half_of(next_left, 0)[...] = half_of(part(left), 0)[...]
    yield
    one.wait_recv()
    add_into(half_of(next_right, 0), half_of(part(right), 0), half_of(first, 0))
    three = sems.copy(next_right, last_left, step_along(axis, 1))
    three.start()
    two.wait_recv()
    add_into(half_of(next_left, 1), half_of(part(left), 1), half_of(first, 1))
    four = sems.copy(next_left, last_right, step_along(axis, -1))
    four.start()
    yield
    three.wait_recv()
    four.wait_recv()
    add_into(out, part(me), last_left, last_right)
    for copy in (one, two, three, four):
        copy.wait_send()


def reduce_direct(sems, axis, part, inbox, out):
    copies = [
        sems.copy(part(shifted(axis, d)), inbox.at[d - 1], step_along(axis, d)) for d in (1, 3, 2)
    ]
    for copy in copies:
        copy.start()
    yield
    for copy in copies:
        copy.wait_recv()
    add_into(out, part(shifted(axis, 0)), *(inbox.at[d] for d in range(3)))
    for copy in copies:
        copy.wait_send()


def chip_reduce(sems, order, source, scratch):
    scratch = list(scratch)
    if len(scratch) == 2 * len(order):
        total = None
    else:
        bufs, total = scratch[:5], scratch[5]
        yield from reduce_ring(sems, order[0], source, bufs, total)
        del scratch[:6]
    for axis in order[0 if total is None else 1 :]:
        inbox, out = scratch[:2]
        del scratch[:2]
        part = source if total is None else (lambda i, t=total: t.at[i])
        yield from reduce_direct(sems, axis, part, inbox, out)
        total = out


def reduce_scratch(order, tail, ring=True):
    count = len(order)
    lead = (RING,) * (count - 1)
    scratch = [VM(lead + tail, bf16) for _ in range(6)] if ring else []
    for number in range(1 if ring else 0, count):
        shape = (RING,) * (count - 1 - number) + tail
        scratch.append(VM((3,) + shape, bf16))
        scratch.append(VM(shape, f32 if number == count - 1 else bf16))
    return scratch


def remote_call(kernel, outs, ins, scratch, copies, collective, *args):
    return pl.pallas_call(
        kernel,
        out_shape=[jax.ShapeDtypeStruct(shape, dtype) for shape, dtype, _ in outs],
        in_specs=[pl.BlockSpec(memory_space=space) for space in ins],
        out_specs=[pl.BlockSpec(memory_space=space) for _, _, space in outs],
        scratch_shapes=list(scratch)
        + [pltpu.SemaphoreType.DMA((copies,)), pltpu.SemaphoreType.DMA((copies,))],
        compiler_params=pltpu.CompilerParams(
            collective_id=collective, has_side_effects=True, vmem_limit_bytes=60 << 20
        ),
    )(*args)


def mm(left, right, dims):
    return lax.dot_general(left, right, ((dims[0], dims[1]), ((), ())), preferred_element_type=f32)


NN, NT, TN = ((1,), (0,)), ((1,), (1,)), ((0,), (0,))


def inverse_norm(values):
    return lax.rsqrt(jnp.sum(values * values, axis=-1, keepdims=True) / D + norm_eps)


def norm_back(values, scale, delta, gain):
    turned = delta * gain
    along = jnp.sum(turned * values, axis=-1, keepdims=True) / D
    return scale * turned - values * (scale * scale * scale) * along


def roll_halves(values):
    lane = lax.broadcasted_iota(jnp.int32, values.shape, 1)
    low = (lane & (HEAD_DIM - 1)) < HEAD_DIM // 2
    return jnp.where(
        low, pltpu.roll(values, 2 * HEAD_DIM - HEAD_DIM // 2, 1), pltpu.roll(values, HEAD_DIM // 2, 1)
    )


def pick(matrix, rows, dims=NN):
    return mm(matrix, rows, dims).astype(bf16)


def deal_line(sems, rows, out, turn_ref, held):
    x, c = lax.axis_index("x"), lax.axis_index("c")
    width = rows.shape[-1]
    held[...] = pick(turn_ref[...], rows).reshape(RING, 2, 16, width)
    copies = [sems.copy(held.at[peer["x"], peer["c"]], out.at[x, c], peer) for peer in line_peers()]
    for copy in copies:
        copy.start()
    out[x, c] = held[x, c]
    yield
    for copy in copies:
        copy.wait()


def deal_plane(sems, rows_ref, out, turn_ref, swap_ref, given, taken):
    width = out.shape[-1]
    rows = pick(turn_ref[...], rows_ref[...].reshape(DEVICES, width), TN)
    for number, axis in enumerate("yz"):
        at = lax.axis_index(axis)
        given[number] = rows.reshape(RING, 32, width)
        copies = [
            sems.copy(
                given.at[number, shifted(axis, d)], taken.at[number, at], step_along(axis, d)
            )
            for d in (1, 3, 2)
        ]
        for copy in copies:
            copy.start()
        taken[number, at] = given[number, at]
        yield
        for copy in copies:
            copy.wait()
        rows = pick(swap_ref[...], taken[number].reshape(DEVICES, width))
    out[...] = rows


def eight(rows):
    return jnp.concatenate([rows, jnp.zeros((1, rows.shape[1]), f32)], axis=0)


def spread_kernel(
    tokens_ref,
    cotangent_ref,
    in_ref,
    out_ref,
    gains_ref,
    gate_ref,
    down_ref,
    turn_ref,
    pair_ref,
    line_ref,
    here_ref,
    x_line,
    up_line,
    att,
    gate,
    down,
    att_in,
    gate_in,
    x_held,
    up_held,
    send,
    recv,
):
    x, c = lax.axis_index("x"), lax.axis_index("c")
    me = device_number()
    target = lax.rem(me, 16) * 8 + me // 16
    source = lax.rem(me, 8) * 16 + me // 8
    line = line_peers()
    in_weight, out_weight = eight(in_ref[...]), eight(out_ref[...])
    none = jnp.zeros((8, HEAD_DIM), f32)
    gains = jnp.concatenate([gains_ref[...], jnp.zeros((2, 121), f32)], axis=1)
    before, after = jnp.zeros((HEAD_DIM, 128), f32), jnp.zeros((HEAD_DIM - 2, 128), f32)
    gains = jnp.concatenate([before, gains, after], axis=0).T[:8]
    for h in range(KV_HEADS):
        k_at, v_at = D + HEAD_DIM * h, D + HEAD_DIM * (KV_HEADS + h)
        first, six, last = HALF_Q * h, HALF_Q * h + HEADS_6, HALF_Q * (h + 1)
        att[h] = jnp.concatenate(
            [
                in_weight[:, first:six],
                out_weight[:, first:six],
                in_weight[:, six:last],
                in_weight[:, k_at : k_at + HEAD_DIM],
                in_weight[:, v_at : v_at + HEAD_DIM],
                none,
                out_weight[:, six:last],
                none,
            ],
            axis=1,
        )
        att[h, :, pl.ds(LAST, 128)] += gains
    gate_weight = eight(gate_ref[...])
    none = jnp.zeros((8, HID - SLICE), f32)
    for rank in range(RANKS):
        at = SLICE * rank
        piece = [
            jnp.concatenate([gate_weight[:, at : at + SLICE], none], axis=1),
            jnp.concatenate([gate_weight[:, FF + at : FF + at + SLICE], none], axis=1),
        ]
        gate[rank // 2, rank % 2] = jnp.concatenate(piece, axis=0).astype(bf16)
    down[...] = jnp.concatenate(
        [down_ref[...], jnp.zeros((DOWN_PAD - DOWN_ROWS, D), f32)], axis=0
    ).astype(bf16)
    greet(line, target, source)
    sems = Sems(send, recv)
    swap = sems.copy(att.at[1 - c], att_in, step_along("c", 1))
    swap.start()
    deals = [
        deal_line(sems, tokens_ref[...], x_line, turn_ref, x_held),
        deal_line(sems, cotangent_ref[...], up_line, turn_ref, up_held),
    ]
    next(deals[0])
    shares = [sems.copy(gate.at[peer["x"], peer["c"]], gate_in.at[x, c], peer) for peer in line]
    for copy in shares:
        copy.start()
    move = sems.copy(down, here_ref, place(target))
    stay = sems.local(down, here_ref)

    @pl.when(target != me)
    def _():
        move.start()

    @pl.when(target == me)
    def _():
        stay.start()

    next(deals[1])
    gate_in[x, c] = gate[x, c]
    swap.wait()
    own, other = att[c], att_in[...]
    first = jnp.where(c == 0, own, other)
    second = jnp.where(c == 0, other, own)
    pair_ref[...] = jnp.concatenate([first, second], axis=0).astype(bf16)
    for copy in shares:
        copy.wait()
    for i in range(RING):
        one, two = gate_in[i, 0].astype(f32), gate_in[i, 1].astype(f32)
        left = jnp.concatenate([one[:8], two[:8]], axis=0)
        right = jnp.concatenate([one[8:], two[8:]], axis=0)
        line_ref[i] = jnp.concatenate([left, right], axis=1).astype(bf16)
    together(*deals)

    @pl.when(target != me)
    def _():
        move.wait()

    @pl.when(target == me)
    def _():
        stay.wait()


def spread(*args):
    rows = (RING, 2, 16, D)
    return remote_call(
        spread_kernel,
        [
            ((16, ATT_COLS), bf16, VM),
            ((RING, 16, 2 * HID), bf16, VM),
            ((DOWN_PAD, D), bf16, VM),
            (rows, bf16, VM),
            (rows, bf16, VM),
        ],
        [VM] * 8,
        [
            VM((2, 8, ATT_COLS), f32),
            VM((RING, 2, 16, HID), bf16),
            VM((DOWN_PAD, D), bf16),
            VM((8, ATT_COLS), f32),
            VM((RING, 2, 16, HID), bf16),
            VM(rows, bf16),
            VM(rows, bf16),
        ],
        32,
        0,
        *args,
    )


KEY_SPLITS = (("xyz", 0, 96), ("zxy", 96, 96), ("yzx", 192, 64))
ROW_SPLITS = (("yzx", 0, 96), ("zxy", 96, 96), ("xyz", 192, 64))
IN_SPLITS = (("xyz", 0, 256), ("yzx", LATE, 256), ("zxy", 256, 128), ("zxy", LAST, 128))
OUT_SPLITS = (("xyz", HEADS_6, 128), ("yzx", HEADS_6 + 128, 128), ("zxy", HEADS_6 + 256, 128))
EARLY_SPLITS = (("xyz", 0, 256), ("yzx", 256, 256), ("zxy", 512, 256))
LATE_SPLITS = (("xyz", LATE, 128), ("yzx", LATE + 128, 128), ("zxy", LAST, 128))


def project_kernel(
    x_line,
    up_in,
    pair_ref,
    turn_ref,
    swap_ref,
    wide_ref,
    order_ref,
    cos_ref,
    sin_ref,
    q_ref,
    normed_ref,
    x_wide_ref,
    gains_ref,
    att_ref,
    kv_first,
    kv_second,
    kv_third,
    up_line,
    x_both,
    up_own,
    wide,
    x_given,
    x_taken,
    up_given,
    up_taken,
    *rest,
):
    cut, (send, recv) = rest[:-2], rest[-2:]
    c = lax.axis_index("c")
    splits = IN_SPLITS + OUT_SPLITS
    for (order, first, lanes), buf in zip(splits, cut):
        buf[own_place(reversed(order))] = pair_ref[:, pl.ds(first, lanes)]
    sems = Sems(send, recv)
    wide_here = sems.fetch(wide_ref, wide)
    greet(axis_peers("yzxc"))

    def settle_columns(number):
        order, first, lanes = splits[number]
        for chip, spot in enumerate(natural(order[::-1])):
            att_ref[chip, :, pl.ds(first, lanes)] = cut[number][spot]

    def advance(*steps):
        for step in steps:
            next(step, None)

    gathers = [chip_gather(sems, split[0], buf) for split, buf in zip(splits, cut)]
    weights, others = gathers[: len(IN_SPLITS)], gathers[len(IN_SPLITS) :]
    deal_x = deal_plane(sems, x_line, x_both.at[c], turn_ref, swap_ref, x_given, x_taken)
    deal_up = deal_plane(sems, up_in, up_own, turn_ref, swap_ref, up_given, up_taken)
    advance(deal_x, *weights)
    advance(deal_x, *weights)
    advance(deal_x)
    swap = sems.copy(x_both.at[c], x_both.at[c], step_along("c", 1))
    swap.start()
    advance(*weights)
    advance(*others)
    advance(deal_up)
    swap.wait()
    wide_here.wait()
    x_wide = mm(x_both[...].reshape(CHIP, D), wide[...], NN)
    x_wide_ref[...] = x_wide.astype(bf16).reshape(2, LOCAL, WIDE)
    scaled = x_wide * inverse_norm(x_wide)
    advance(*weights)
    advance(*others)
    advance(deal_up)
    together(*weights)
    advance(deal_up)
    up_line[own_place("xc")] = up_own[...]
    advance(*others)
    for number in range(len(IN_SPLITS)):
        settle_columns(number)

    gains = att_ref[:, :, pl.ds(LAST, 128)].reshape(WIDE, 128).astype(f32).T
    gains_ref[...] = gains[GAIN_AT - LAST : GAIN_AT - LAST + 8]
    normed = (scaled * gains_ref[0:1]).astype(bf16)
    normed_ref[...] = normed
    joined = jnp.concatenate(
        [
            mm(normed, att_ref[:, :, pl.ds(0, HEADS_6)].reshape(WIDE, HEADS_6), NN),
            mm(normed, att_ref[:, :, pl.ds(LATE, 256)].reshape(WIDE, 256), NN),
        ],
        axis=1,
    )
    cosine, sine = cos_ref[...], sin_ref[...]
    turned = []
    for tile in range(4):
        values = joined[:, 128 * tile : 128 * (tile + 1)]
        turned.append((values * cosine + roll_halves(values) * sine).astype(bf16))
    queries = jnp.concatenate(turned, axis=1)
    q_ref[...] = (queries * jnp.asarray(HEAD_DIM ** (-0.5), bf16)).reshape(2, LOCAL, OUT_COLS)
    keys_values = jnp.concatenate(
        [turned[3][:, HEAD_DIM:], joined[:, OUT_COLS : OUT_COLS + HEAD_DIM].astype(bf16)], axis=1
    )
    keys_values = pick(order_ref[...], keys_values)
    kvs = (kv_first, kv_second, kv_third)
    for (order, first, count), kv in zip(KEY_SPLITS, kvs):
        kv[own_place(reversed(order))] = keys_values[first : first + count]
    together(
        *(chip_gather(sems, split[0], kv) for split, kv in zip(KEY_SPLITS, kvs)),
        *others,
        in_turn(gather_line(sems, up_line)),
    )
    for number in range(len(IN_SPLITS), len(splits)):
        settle_columns(number)


def project(*args):
    return remote_call(
        project_kernel,
        [
            ((2, LOCAL, OUT_COLS), bf16, VM),
            ((CHIP, WIDE), bf16, VM),
            ((2, LOCAL, WIDE), bf16, VM),
            ((8, WIDE), f32, VM),
            ((CHIPS, 16, ATT_COLS), bf16, VM),
            *(
                ((RING, RING, RING, count, 2 * HEAD_DIM), bf16, VM)
                for _, _, count in KEY_SPLITS
            ),
            ((RING, 2, LOCAL, D), bf16, VM),
        ],
        [VM] * 5 + [ANY] + [VM] * 3,
        [
            VM((2, LOCAL, D), bf16),
            VM((LOCAL, D), bf16),
            VM((D, WIDE), bf16),
        ]
        + [VM((2, RING, 32, D), bf16)] * 4
        + [VM((RING, RING, RING, 16, lanes), bf16) for _, _, lanes in IN_SPLITS + OUT_SPLITS],
        128,
        1,
        *args,
    )


def begins(starts_ref, position):
    begin = jnp.zeros_like(position)
    for number in range(DOCS):
        start = starts_ref[number]
        begin = jnp.maximum(begin, jnp.where(position >= start, start, 0))
    return begin


def query_places(block, chip_ref, shape, axis):
    index = lax.broadcasted_iota(jnp.int32, shape, axis)
    row = block * SPAN + ((index >> 4) & 1) * HALF + (index & (HALF - 1))
    return row * DEVICES + chip_ref[0] + ((index >> 3) & 1)


def key_places(shape, axis):
    index = lax.broadcasted_iota(jnp.int32, shape, axis)
    return (index & (HALF - 1)) * DEVICES + (index >> 4) * 2 + ((index >> 3) & 1)


def first_place(tile, piece):
    return tile * TILE + piece // 2 * HALF_TILE + piece % 2 * (PIECE // SPAN * 2)


def tile_range(block, starts_ref, chip_ref):
    first = block * TILE + chip_ref[0]
    last = first + (SPAN - 1) * DEVICES + 1
    low = begins(starts_ref, first) // HALF_TILE
    full = (begins(starts_ref, last) + (TILE - 1)) // TILE
    return low, jnp.minimum(full, block)


def over_tiles(block, starts_ref, chip_ref, step):
    low, full = tile_range(block, starts_ref, chip_ref)
    every, upper = range(PIECES), range(PIECES // 2, PIECES)

    @pl.when(((low & 1) == 1) & (low // 2 < block))
    def _():
        step(low // 2, True, upper, False)

    @pl.loop((low + 1) // 2, full)
    def _(tile):
        step(tile, True, every, False)

    @pl.loop(full, block)
    def _(tile):
        step(tile, False, every, False)

    step(block, True, range(PIECES // 2), False)
    step(block, True, upper, True)


def stack_heads(rows):
    parts = []
    for half in range(2):
        kept = rows[:, HALF * half : HALF * (half + 1)]
        for h in range(GROUP):
            part = kept[:, :, HEAD_DIM * h : HEAD_DIM * (h + 1)]
            parts.append(part.reshape(SPAN, HEAD_DIM))
    return jnp.concatenate(parts, axis=0)


def unstack_heads(stacked):
    halves = []
    for half in range(2):
        parts = [
            stacked[HALF_ROWS * half + SPAN * h : HALF_ROWS * half + SPAN * (h + 1)]
            for h in range(GROUP)
        ]
        rows = jnp.concatenate(parts + [jnp.zeros_like(parts[0])], axis=1)
        halves.append(rows.reshape(2, HALF, OUT_COLS))
    return jnp.concatenate(halves, axis=1)


def pad_halves(rows):
    gap = jnp.zeros((QPAD // 2 - HALF_ROWS, rows.shape[1]), rows.dtype)
    return jnp.concatenate([rows[:HALF_ROWS], gap, rows[HALF_ROWS:], gap], axis=0)


def skip_gaps(rows):
    return jnp.concatenate([rows[:HALF_ROWS], rows[QPAD // 2 : QPAD // 2 + HALF_ROWS]], axis=0)


PIECE = 512
PIECES = TILE // PIECE


def seen(places, lowest, highest, first):
    times = [whole // part for whole, part in zip(places.shape, lowest.shape)]

    def spread_out(rows):
        for axis, count in enumerate(times):
            if count > 1:
                rows = jnp.concatenate([rows] * count, axis=axis)
        return rows

    return (places <= spread_out(highest - first)) & (places >= spread_out(lowest - first))


def attend_kernel(
    starts_ref,
    chip_ref,
    q_ref,
    kv_first,
    kv_second,
    kv_third,
    mixed_ref,
    out_ref,
    lse_ref,
    keys_out,
    turned_out,
    m_ref,
    acc_ref,
    values_ref,
    turned_ref,
):
    block = pl.program_id(0)
    for (order, first, count), kv in zip(KEY_SPLITS, (kv_first, kv_second, kv_third)):
        first, count = first // (2 * SPAN), count // (2 * SPAN)

        @pl.when((block >= first) & (block < first + count))
        def _(order=order, kv=kv):
            lane = lax.broadcasted_iota(jnp.int32, (HALF_TILE, 2 * HEAD_DIM), 1)
            none = jnp.zeros((HEAD_DIM, HALF_TILE), bf16)
            for half in range(2):
                at = pl.ds(SPAN * half, SPAN)
                keys = jnp.concatenate([kv[(*spot, at)] for spot in natural(order[::-1])], axis=0)
                turned = jnp.concatenate([keys.T[:HEAD_DIM], none], axis=0)
                keys_out[half] = keys
                turned_out[half] = turned
                turned_ref[2 * block + half] = turned
                values_ref[2 * block + half] = jnp.where(lane < HEAD_DIM, jnp.ones_like(keys), keys)

    m_ref[...] = jnp.full(m_ref.shape, masked_score, f32)
    acc_ref[...] = jnp.zeros(acc_ref.shape, f32)
    query = stack_heads(q_ref[...].astype(f32)).astype(bf16)
    row = lax.broadcasted_iota(jnp.int32, query.shape, 0)
    lane = lax.broadcasted_iota(jnp.int32, query.shape, 1)
    slot = (row & (SPAN - 1)) + jnp.where(row >= HALF_ROWS, SPAN, 0)
    query = jnp.concatenate([query, jnp.where(slot == lane, 1.0, 0.0).astype(bf16)], axis=1)
    none = jnp.zeros((HEAD_DIM - 2 * SPAN, PIECE), bf16)
    places = key_places((2 * SPAN, PIECE), 1)
    pos = query_places(block, chip_ref, (2 * SPAN, 128), 0)
    start = begins(starts_ref, pos)

    def tile_step(tile, masked, pieces, upper):
        rows = pl.ds(HALF_ROWS, HALF_ROWS) if upper else pl.ds(0, QROWS)
        asked = query[HALF_ROWS:] if upper else query
        found = []
        for piece in pieces:
            half, at = 2 * tile + piece // 2, pl.ds(piece % 2 * PIECE, PIECE)
            if masked:
                allowed = seen(places, start, pos, first_place(tile, piece))
                table = jnp.where(allowed, 0.0, masked_score).astype(bf16)
                keys = jnp.concatenate([turned_ref[half, pl.ds(0, HEAD_DIM), at], table, none], axis=0)
            else:
                keys = turned_ref[half, :, at]
            found.append(mm(asked, keys, NN))
        before = m_ref[rows]
        highest = found[0]
        for scores in found[1:]:
            highest = jnp.maximum(highest, scores)
        highest = jnp.max(highest, axis=1, keepdims=True)
        highest = jnp.maximum(before, jnp.broadcast_to(highest, before.shape))
        m_ref[rows] = highest
        total = acc_ref[rows] * jnp.exp(before - highest)
        level = jnp.concatenate([highest] * (PIECE // 128), axis=1)
        for piece, scores in zip(pieces, found):
            weights = jnp.exp(scores - level).astype(bf16)
            values = values_ref[2 * tile + piece // 2, pl.ds(piece % 2 * PIECE, PIECE)]
            total = total + mm(weights, values, NN)
        acc_ref[rows] = total

    over_tiles(block, starts_ref, chip_ref, tile_step)
    total = jnp.broadcast_to(acc_ref[:, 0:1], acc_ref.shape)
    out = acc_ref[...] / total
    out_ref[0] = pad_halves(out)
    mixed_ref[...] = unstack_heads(out[:, HEAD_DIM:]).astype(bf16)
    lse_ref[0] = pad_halves(m_ref[...] + jnp.log(total)).T[0:8]


def row_block(lanes):
    return pl.BlockSpec((2, SPAN, lanes), lambda b, *_: (0, b, 0))


def one_block(rows, lanes):
    return pl.BlockSpec((1, rows, lanes), lambda b, *_: (b, 0, 0))


def two_halves(rows, lanes):
    return pl.BlockSpec((2, rows, lanes), lambda b, *_: (b, 0, 0))


def tile_block(first, count):
    first, count = first // (2 * SPAN), count // (2 * SPAN)
    return pl.BlockSpec(
        (RING, RING, RING, 2 * SPAN, 2 * HEAD_DIM),
        lambda b, *_: (0, 0, 0, jnp.clip(b - first, 0, count - 1), 0),
    )


def whole(*shape):
    return pl.BlockSpec(shape, lambda b, *_: (0,) * len(shape))


def attend(starts, chip, query, *keys):
    pairs = BLOCKS * 2 * QROWS * TILE
    return pl.pallas_call(
        attend_kernel,
        out_shape=[
            jax.ShapeDtypeStruct((2, LOCAL, OUT_COLS), bf16),
            jax.ShapeDtypeStruct((BLOCKS, QPAD, 2 * HEAD_DIM), f32),
            jax.ShapeDtypeStruct((BLOCKS, 8, QPAD), f32),
            jax.ShapeDtypeStruct((2 * BLOCKS, HALF_TILE, 2 * HEAD_DIM), bf16),
            jax.ShapeDtypeStruct((2 * BLOCKS, 2 * HEAD_DIM, HALF_TILE), bf16),
        ],
        grid_spec=pltpu.PrefetchScalarGridSpec(
            num_scalar_prefetch=2,
            grid=(BLOCKS,),
            in_specs=[row_block(OUT_COLS), *(tile_block(*split[1:]) for split in KEY_SPLITS)],
            out_specs=[
                row_block(OUT_COLS),
                one_block(QPAD, 2 * HEAD_DIM),
                one_block(8, QPAD),
                two_halves(HALF_TILE, 2 * HEAD_DIM),
                two_halves(2 * HEAD_DIM, HALF_TILE),
            ],
            scratch_shapes=[
                VM((QROWS, 2 * HEAD_DIM), f32),
                VM((QROWS, 2 * HEAD_DIM), f32),
                VM((2 * BLOCKS, HALF_TILE, 2 * HEAD_DIM), bf16),
                VM((2 * BLOCKS, 2 * HEAD_DIM, HALF_TILE), bf16),
            ],
        ),
        compiler_params=pltpu.CompilerParams(
            dimension_semantics=("arbitrary",), vmem_limit_bytes=56 << 20
        ),
        cost_estimate=pl.CostEstimate(
            flops=pairs * 512, bytes_accessed=5 << 20, transcendentals=pairs
        ),
    )(starts, chip, query, *keys)


def three_terms(numbers):
    first = numbers.astype(bf16)
    rest = numbers - first.astype(f32)
    second = rest.astype(bf16)
    third = (rest - second.astype(f32)).astype(bf16)
    return jnp.concatenate([first, second, third], axis=0)


def attend_back_kernel(
    starts_ref,
    chip_ref,
    q_ref,
    branch_ref,
    six_ref,
    last_ref,
    keys_in,
    turned_in,
    out_ref,
    lse_ref,
    dq_ref,
    dkv_first,
    dkv_second,
    dkv_third,
    keys_ref,
    turned_ref,
    sum_ref,
    delta_ref,
    dq_acc,
):
    block = pl.program_id(0)
    own = pl.ds(2 * block, 2)
    keys_ref[own] = keys_in[...]
    turned_ref[own] = turned_in[...]
    sum_ref[own] = jnp.zeros((2, HALF_TILE, 2 * HEAD_DIM), f32)

    @pl.when(block == 0)
    def _():
        branch = branch_ref[...].reshape(CHIP, WIDE)
        delta = mm(branch, six_ref[...], NN)
        delta_ref[:, :, pl.ds(0, HEADS_6)] = delta.astype(bf16).reshape(2, LOCAL, HEADS_6)
        delta = mm(branch, last_ref[...], NN)
        delta_ref[:, :, pl.ds(HEADS_6, 128)] = delta.astype(bf16).reshape(2, LOCAL, 128)

    dq_acc[...] = jnp.zeros(dq_acc.shape, f32)
    mine = pl.ds(pl.multiple_of(block * SPAN, SPAN), SPAN)
    query = pad_halves(stack_heads(q_ref[...].astype(f32)).astype(bf16))
    delta_out = pad_halves(stack_heads(delta_ref[:, mine, :].astype(f32)).astype(bf16))
    none = jnp.zeros_like(query)
    delta_out = jnp.concatenate([none, delta_out], axis=1)
    both = jnp.concatenate([jnp.concatenate([query, none], axis=1), delta_out], axis=0)
    inner = jnp.sum((delta_out.astype(f32) * out_ref[0]).T, axis=0, keepdims=True)
    slot = lax.broadcasted_iota(jnp.int32, (2 * SPAN, 2 * QPAD), 0)
    lane = lax.broadcasted_iota(jnp.int32, (2 * SPAN, 2 * QPAD), 1)
    within = lane & (QPAD // 2 - 1)
    asked = (within & (SPAN - 1)) + ((lane >> 7) & 1) * SPAN
    which = (asked == slot) & (within < HALF_ROWS) & (lane < QPAD)
    which = jnp.where(which, 1.0, 0.0).astype(bf16)
    taken = three_terms(jnp.concatenate([-lse_ref[0, 0:1], -inner], axis=1))
    rest = jnp.zeros((2 * HEAD_DIM - 2 * SPAN - 3, 2 * QPAD), bf16)
    both_turned = jnp.concatenate([both.T, which, taken, rest], axis=0)
    half = QPAD // 2
    upper_turned = jnp.concatenate(
        [both_turned[:, half:QPAD], both_turned[:, QPAD + half :]], axis=1
    )
    upper_both = jnp.concatenate([both[half:QPAD], both[QPAD + half :]], axis=0)
    lane = lax.broadcasted_iota(jnp.int32, (PIECE, 2 * HEAD_DIM), 1)
    ones = jnp.where((lane >= 2 * SPAN) & (lane < 2 * SPAN + 3), 1.0, 0.0)
    places = key_places((PIECE, 2 * HEAD_DIM), 0)
    pos = query_places(block, chip_ref, (8, 2 * HEAD_DIM), 1)
    start = begins(starts_ref, pos)
    slot_lane = lax.broadcasted_iota(jnp.int32, pos.shape, 1) < 2 * SPAN
    far = jnp.int32(1 << 20)
    pos, start = jnp.where(slot_lane, pos, far), jnp.where(slot_lane, start, -far)

    def tile_step(tile, masked, pieces, upper):
        turned, rows = (upper_turned, upper_both) if upper else (both_turned, both)
        lanes = pl.ds(half, half) if upper else pl.ds(0, QPAD)
        width = half if upper else QPAD

        def product(piece):
            keys = keys_ref[2 * tile + piece // 2, pl.ds(piece % 2 * PIECE, PIECE)]
            beside = ones
            if masked:
                allowed = seen(places, start, pos, first_place(tile, piece))
                beside = jnp.where(allowed, ones, masked_score)
            return mm(jnp.concatenate([keys, beside.astype(bf16)], axis=1), turned, NN)

        ahead = product(pieces[0])
        total = dq_acc[:, lanes]
        for piece in pieces:
            raw = ahead
            if piece + 1 in pieces:
                ahead = product(piece + 1)
            scores, delta = raw[:, :width], raw[:, width:]
            weights = jnp.exp(scores)
            delta = (weights * delta).astype(bf16)
            joined = jnp.concatenate([delta, weights.astype(bf16)], axis=1)
            at = pl.ds(piece % 2 * PIECE, PIECE)
            sum_ref[2 * tile + piece // 2, at] += mm(joined, rows, NN)
            total = total + mm(turned_ref[2 * tile + piece // 2, :, at], delta, NN)
        dq_acc[:, lanes] = total

    over_tiles(block, starts_ref, chip_ref, tile_step)
    delta_q = skip_gaps(dq_acc[...].T)[:, :HEAD_DIM] * HEAD_DIM ** (-0.5)
    dq_ref[...] = unstack_heads(delta_q)

    @pl.when(block == BLOCKS - 1)
    def _():
        for (order, first, count), dkv in zip(ROW_SPLITS, (dkv_first, dkv_second, dkv_third)):

            @pl.loop(0, count // SPAN)
            def _(number, order=order, first=first, dkv=dkv):
                at = pl.ds(pl.multiple_of(number * SPAN, SPAN), SPAN)
                sums = sum_ref[first // SPAN + number].astype(bf16)
                for chip, spot in enumerate(natural(order)):
                    dkv[(*spot, at)] = sums[SPAN * chip : SPAN * (chip + 1)]


def attend_back(starts, chip, query, branch, att, keys, turned, out, lse):
    pairs = BLOCKS * 2 * QROWS * TILE
    sums = [(RING, RING, RING, count, 2 * HEAD_DIM) for _, _, count in ROW_SPLITS]
    return pl.pallas_call(
        attend_back_kernel,
        out_shape=[
            jax.ShapeDtypeStruct((2, LOCAL, OUT_COLS), f32),
            *(jax.ShapeDtypeStruct(shape, bf16) for shape in sums),
        ],
        grid_spec=pltpu.PrefetchScalarGridSpec(
            num_scalar_prefetch=2,
            grid=(BLOCKS,),
            in_specs=[
                row_block(OUT_COLS),
                whole(2, LOCAL, WIDE),
                pl.BlockSpec((WIDE, HEADS_6), lambda b, *_: (0, 1)),
                pl.BlockSpec((WIDE, 128), lambda b, *_: (0, LAST // 128)),
                two_halves(HALF_TILE, 2 * HEAD_DIM),
                two_halves(2 * HEAD_DIM, HALF_TILE),
                one_block(QPAD, 2 * HEAD_DIM),
                one_block(8, QPAD),
            ],
            out_specs=[row_block(OUT_COLS), *(whole(*shape) for shape in sums)],
            scratch_shapes=[
                VM((2 * BLOCKS, HALF_TILE, 2 * HEAD_DIM), bf16),
                VM((2 * BLOCKS, 2 * HEAD_DIM, HALF_TILE), bf16),
                VM((2 * BLOCKS, HALF_TILE, 2 * HEAD_DIM), f32),
                VM((2, LOCAL, OUT_COLS), bf16),
                VM((2 * HEAD_DIM, QPAD), f32),
            ],
        ),
        compiler_params=pltpu.CompilerParams(
            dimension_semantics=("arbitrary",), vmem_limit_bytes=56 << 20
        ),
        cost_estimate=pl.CostEstimate(
            flops=pairs * 1280, bytes_accessed=12 << 20, transcendentals=pairs
        ),
    )(starts, chip, query, branch, att, att, keys, turned, out, lse)


def feed_kernel(
    mixed_ref,
    att_ref,
    x_ref,
    gains_ref,
    gate_ref,
    down_ref,
    up_ref,
    wide_ref,
    pack_ref,
    mid_ref,
    dmid_ref,
    both_ref,
    dgain_ref,
    part_ref,
    grad_gate_ref,
    grad_down_ref,
    w_out,
    x_own,
    gate,
    down,
    up,
    wide,
    pack,
    given,
    other,
    normed,
    delta_all,
    hidden_all,
    dn,
    pair_in,
    reduced,
    inbox,
    own_sum,
    w_down,
    w_down_wide,
    send,
    recv,
):
    x, c = lax.axis_index("x"), lax.axis_index("c")
    sibling = step_along("c", 1)
    sems = Sems(send, recv)
    first = [
        sems.fetch(att_ref.at[:, pl.ds(HEADS_6, HEADS_6)], w_out.at[:, pl.ds(0, HEADS_6)]),
        sems.fetch(att_ref.at[:, pl.ds(LAST, 128)], w_out.at[:, pl.ds(HEADS_6, 128)]),
        sems.fetch(x_ref.at[c], x_own),
    ]
    later = [
        sems.fetch(down_ref, down),
        sems.fetch(pack_ref, pack),
        sems.fetch(wide_ref, wide),
        sems.fetch(gate_ref, gate),
        sems.fetch(up_ref, up),
    ]
    greet(axis_peers("xc"))
    for copy in first:
        copy.wait()

    given[...] = mm(mixed_ref[1 - c], w_out[...], NT)
    swap = sems.copy(given, other, sibling)
    swap.start()
    mid = x_own[...].astype(f32) + mm(mixed_ref[c], w_out[...], NT)
    swap.wait()
    mid = mid + other[...]
    mid_ref[...] = mid
    normed[x, c] = (mid * inverse_norm(mid) * gains_ref[1:2]).astype(bf16)
    start_line, own_pair, relay, right_pair, relay_far, far_pair, close_line = gather_line(sems, normed)
    arrivals = (own_pair, relay, right_pair, far_pair)
    start_line()
    for copy in later:
        copy.wait()
    w_down[...] = mm(pack[...], down[...], NN).astype(bf16)
    w_down_wide[...] = mm(w_down[...], wide[...], NN).astype(bf16)

    deltas = (0, 3, 1, 2)
    swaps = [
        sems.copy(dn.at[shifted("x", d), 1 - c], pair_in.at[k], sibling)
        for k, d in enumerate(deltas)
    ]
    sends = [
        sems.copy(reduced.at[k], inbox.at[k], step_along("x", deltas[k + 1])) for k in range(3)
    ]

    def finish(k):
        swaps[k].wait_recv()
        total = dn[shifted("x", deltas[k]), c].astype(f32) + pair_in[k].astype(f32)
        if k == 0:
            own_sum[...] = total
        else:
            reduced[k - 1] = total.astype(bf16)
            sends[k - 1].start()

    def chunk(at):
        rows = normed[at].reshape(CHIP, WIDE)
        joined = mm(rows, gate[...], NN)
        gate_part, above = joined[:, :HID], joined[:, HID:]
        sig = 1.0 / (1.0 + jnp.exp(-gate_part))
        silu = gate_part * sig
        hidden = (silu * above).astype(bf16)
        hidden_all[at] = hidden
        delta = mm(up[at].reshape(CHIP, D), w_down[...], NT)
        delta_gate = (delta * above * sig * (1.0 + gate_part * (1.0 - sig))).astype(bf16)
        delta_above = (delta * silu).astype(bf16)
        delta_all[at, :, pl.ds(0, HID)] = delta_gate
        delta_all[at, :, pl.ds(HID, HID)] = delta_above
        dn[at] = mm(delta_all[at], gate[...], NT).astype(bf16).reshape(2, LOCAL, WIDE)
        part_ref[at] = mm(hidden, w_down_wide[...], NN).astype(bf16).reshape(2, LOCAL, WIDE)

    @pl.loop(0, RING)
    def _(step):
        for k in range(RING):

            @pl.when(step == k)
            def _(k=k):
                arrivals[k]()

        delta = jnp.where(step == 1, 3, jnp.where(step > 1, step - 1, 0))
        chunk(lax.rem(x + delta, RING))
        for k in range(RING):

            @pl.when(step == k)
            def _(k=k):
                swaps[k].start()
                if k == 2:
                    relay_far()
                if k:
                    finish(k - 1)

    finish(3)
    close_line()

    @pl.loop(0, RING)
    def _(block):
        at = pl.ds(pl.multiple_of(block * 256, 256), 256)
        total = jnp.zeros((256, 2 * HID), f32)
        for chip in range(RING):
            total = total + mm(normed[chip, :, :, at].reshape(CHIP, 256), delta_all[chip], TN)
        grad_gate_ref[at, :] = total.astype(bf16)

    total = jnp.zeros((HID, D), f32)
    for chip in range(RING):
        total = total + mm(hidden_all[chip], up[chip].reshape(CHIP, D), TN)
    grad_down_ref[...] = mm(pack[...], total.astype(bf16), TN).astype(bf16)

    for copy in sends:
        copy.wait_recv()
    delta = own_sum[...] + inbox[0].astype(f32) + inbox[1].astype(f32) + inbox[2].astype(f32)
    mid = mid_ref[...]
    scale = inverse_norm(mid)
    dgain_ref[...] = jnp.sum(delta * mid * scale, axis=0, keepdims=True)
    upstream = mm(up[x, c], wide[...], NN)
    dmid = upstream + norm_back(mid, scale, delta, gains_ref[1:2])
    dmid_ref[...] = dmid
    both_ref[c] = dmid.astype(bf16)
    share = sems.copy(both_ref.at[c], both_ref.at[c], sibling)
    share.start()
    for copy in swaps + sends:
        copy.wait_send()
    share.wait()


def feed(mixed, att, x_wide, gains, gate, down, up, widen, pack):
    block = (LOCAL, WIDE)
    return remote_call(
        feed_kernel,
        [
            (block, f32, VM),
            (block, f32, VM),
            ((2, *block), bf16, VM),
            ((1, WIDE), f32, VM),
            ((RING, 2, *block), bf16, VM),
            ((WIDE, 2 * HID), bf16, VM),
            ((16 * DOWN_PAD, D), bf16, VM),
        ],
        [VM, ANY, ANY, VM, ANY, ANY, ANY, ANY, ANY],
        [
            VM((WIDE, OUT_COLS), bf16),
            VM(block, bf16),
            VM((WIDE, 2 * HID), bf16),
            VM((16 * DOWN_PAD, D), bf16),
            VM((RING, 2, LOCAL, D), bf16),
            VM((D, WIDE), bf16),
            VM((HID, 16 * DOWN_PAD), bf16),
            VM(block, f32),
            VM(block, f32),
            VM((RING, 2, *block), bf16),
            VM((RING, CHIP, 2 * HID), bf16),
            VM((RING, CHIP, HID), bf16),
            VM((RING, 2, *block), bf16),
            VM((RING, *block), bf16),
            VM((3, *block), bf16),
            VM((3, *block), bf16),
            VM(block, f32),
            VM((HID, D), bf16),
            VM((HID, WIDE), bf16),
        ],
        32,
        2,
        mixed,
        att,
        x_wide,
        gains,
        gate,
        down,
        up,
        widen,
        pack,
    )


DOWN_SPLITS = (("yz", 0, 32), ("zy", 32, 16))


def settle_kernel(
    dkv_first,
    dkv_second,
    dkv_third,
    dq_ref,
    cos_ref,
    sin_ref,
    normed_ref,
    x_ref,
    mixed_ref,
    both_ref,
    att_ref,
    gains_ref,
    dgain_ref,
    gate_ref,
    down_ref,
    part_ref,
    mid_ref,
    dmid_ref,
    wide_ref,
    turn_ref,
    swap_ref,
    output_ref,
    input_grad_ref,
    in_out,
    out_out,
    gains_out,
    gate_out,
    down_out,
    norm_out,
    *rest,
):
    (send, recv), rest = rest[-2:], list(rest[:-2])
    y, z, x, c = (lax.axis_index(axis) for axis in ALL)
    me = device_number()
    sibling = step_along("c", 1)
    target = lax.rem(me, 8) * 16 + me // 8
    source_of = lax.rem(me, 16) * 8 + me // 16
    line = line_peers()
    sems = Sems(send, recv)

    def pop(count):
        taken = rest[:count]
        del rest[:count]
        return taken

    names = ("one", "two", "three", "normed", "both", "mixed", "xs", "att", "part", "down", "gate", "wide")
    kept = dict(zip(names, pop(len(names))))
    sources = (dkv_first, dkv_second, dkv_third, normed_ref, both_ref, mixed_ref, x_ref, att_ref)
    sources += (part_ref, down_ref, gate_ref, wide_ref)
    fetches = {name: sems.fetch(src, kept[name]) for name, src in zip(names, sources)}
    kv_sum, du_all, du_in, att_own, gate_own, down_own = pop(6)
    att_terms = pop(6)
    pair_in, part_own, part_sum, att_pair, gate_in, slots_line, slots = pop(7)
    deal_refs = [pop(4), pop(4)]
    plane = [
        {"y": lax.rem(y + dy, RING), "z": lax.rem(z + dz, RING)}
        for dy in range(RING)
        for dz in range(RING)
        if dy or dz
    ]
    greet(line + plane, target, source_of)

    def reduce_rows(split, dkv, scratch):
        order, first, count = split
        yield from chip_reduce(sems, order, lambda i: dkv.at[i], scratch)
        kv_sum[pl.ds(first, count), :] = scratch[-1][...]

    def advance(*steps):
        for step in steps:
            next(step, None)

    dkvs = [kept[name] for name in names[:3]]
    for name in names[:3]:
        fetches[name].wait()
    rows = [reduce_rows(split, dkv, pop(10)) for split, dkv in zip(ROW_SPLITS, dkvs)]
    advance(*rows)

    def reduce_down(order, first, count, scratch):
        def view(i):
            at = {"y": slice(None), "z": slice(None), order[0]: i}
            return kept["down"].at[at["y"], at["z"], pl.ds(first, count)]

        yield from chip_reduce(sems, order, view, scratch)
        down_own[pl.ds(first, count), :] = scratch[-1][...]

    def reduce_parts(scratch):
        swaps = [sems.copy(kept["part"].at[i, 1 - c], pair_in.at[i], sibling) for i in range(RING)]
        for swap in swaps:
            swap.start()
        yield
        for i in range(RING):
            swaps[i].wait()
            total = kept["part"][i, c].astype(f32) + pair_in[i].astype(f32)
            part_own[i] = total.astype(bf16).reshape(RING, LOCAL // RING, WIDE)
        yield from reduce_ring(sems, "x", lambda i: part_own.at[i], scratch[:5], scratch[5])
        part_sum[...] = scratch[5][...].reshape(LOCAL, WIDE)

    def reduce_att(split, terms, scratch):
        _, first, lanes = split
        yield from chip_reduce(sems, split[0], lambda i: terms.at[i], scratch)
        att_own[:, :, pl.ds(first, lanes)] = scratch[-1][...].reshape(2, 8, lanes)

    def put_terms(split, buf, terms):
        terms = terms.astype(bf16)
        for chip, spot in enumerate(natural(split[0])):
            buf[spot] = terms[16 * chip : 16 * (chip + 1)]

    cosine, sine = cos_ref[...], sin_ref[...]

    def unrotate(values):
        return (values * cosine - roll_halves(values) * sine).astype(bf16)

    delta_q = dq_ref[...].reshape(CHIP, OUT_COLS)
    early = [unrotate(delta_q[:, 128 * tile : 128 * (tile + 1)]) for tile in range(4)]
    early_six = jnp.concatenate(early[:3], axis=1)
    for name in ("normed", "both", "mixed", "att", "xs"):
        fetches[name].wait()
    grad_in = mm(kept["normed"][...], early_six, TN)
    mixed = kept["mixed"][...].reshape(CHIP, OUT_COLS)
    grad_out = mm(kept["both"][...].reshape(CHIP, WIDE), mixed, TN)
    grad_early = jnp.concatenate([grad_in, grad_out[:, :HEADS_6]], axis=1)
    early_terms, late_terms = att_terms[:3], att_terms[3:]
    for split, buf in zip(EARLY_SPLITS, early_terms):
        put_terms(split, buf, grad_early[:, split[1] : split[1] + split[2]])
    earlies = [
        reduce_att(split, buf, pop(10)) for split, buf in zip(EARLY_SPLITS, early_terms)
    ]
    advance(*earlies)
    advance(*rows)
    fetches["part"].wait()
    fetches["down"].wait()
    parts = reduce_parts(pop(6))
    downs = [reduce_down(*split, pop(8)) for split in DOWN_SPLITS]
    advance(parts, *downs)
    delta_normed = mm(early_six, kept["att"][:, :HEADS_6], NT)
    inputs = kept["xs"][...].reshape(CHIP, WIDE).astype(f32)
    scale = inverse_norm(inputs)
    advance(*rows)
    fetches["gate"].wait()
    gate_sum = kept["gate"][0].astype(f32)
    for number in range(1, 16):
        gate_sum = gate_sum + kept["gate"][number].astype(f32)
    gate_own[...] = gate_sum.reshape(RING, 2, 8, 2 * HID)
    shares = [sems.copy(gate_own.at[peer["x"], peer["c"]], gate_in.at[x, c], peer) for peer in line]
    for copy in shares:
        copy.start()
    gate_in[x, c] = gate_own[x, c]
    advance(*rows)
    advance(*earlies, parts)
    together(*rows)

    sums = [
        kv_sum[pl.ds(SPAN * number + 8 * core, 8)] for core in range(2) for number in range(SPAN)
    ]
    sums = jnp.concatenate(sums, axis=0)
    last = jnp.concatenate([delta_q[:, HEADS_6:HALF_Q], sums[:, :HEAD_DIM]], axis=1)
    delta_v = sums[:, HEAD_DIM:].astype(bf16)
    late = jnp.concatenate([unrotate(last), delta_v, jnp.zeros_like(delta_v)], axis=1)
    grad_late = mm(kept["normed"][...], late, TN)
    put_terms(LATE_SPLITS[0], late_terms[0], grad_late[:, :128])
    put_terms(LATE_SPLITS[1], late_terms[1], grad_late[:, 128:])
    lates = [reduce_att(split, buf, pop(6)) for split, buf in zip(LATE_SPLITS, late_terms)]
    advance(*lates[:2])
    delta_normed = delta_normed + mm(late, kept["att"][:, LATE:LAST], NT)
    gain_one = jnp.sum(delta_normed * (inputs * scale), axis=0, keepdims=True)
    row = lax.broadcasted_iota(jnp.int32, (128, WIDE), 0)
    at_gain = GAIN_AT - LAST
    gain_sums = jnp.where(row == at_gain, gain_one, jnp.where(row == at_gain + 1, dgain_ref[...], 0.0))
    put_terms(LATE_SPLITS[2], late_terms[2], grad_out[:, HEADS_6:] + gain_sums.T)
    advance(lates[2])
    du_all[...] = norm_back(inputs, scale, delta_normed, gains_ref[0:1]).reshape(2, LOCAL, WIDE)
    swap = sems.copy(du_all.at[1 - c], du_in, sibling)
    swap.start()
    advance(*downs, *earlies, parts)
    advance(*lates)

    fetches["wide"].wait()
    widen = kept["wide"]

    def deal_back(values, out, held, first, given, taken):
        values = mm(values, widen[...], NN).astype(bf16)
        yield from deal_line(sems, values, first, turn_ref, held)
        yield from deal_plane(sems, first, out, turn_ref, swap_ref, given, taken)

    together(parts)
    result = (mid_ref[...] + part_sum[...]).astype(bf16)
    output = deal_back(result, output_ref, *deal_refs[0])
    advance(output)
    swap.wait()
    input_grad = (dmid_ref[...] + (du_all[c] + du_in[...])).astype(bf16)
    input_back = deal_back(input_grad, input_grad_ref, *deal_refs[1])
    advance(input_back)
    together(*lates, *earlies, *downs, output, input_back)

    pair = sems.copy(att_own.at[1 - c], att_pair.at[c], sibling)
    pair.start()
    move = sems.copy(down_own, down_out, place(target))
    stay = sems.local(down_own, down_out)

    @pl.when(target != me)
    def _():
        move.start()

    @pl.when(target == me)
    def _():
        stay.start()

    lane = lax.broadcasted_iota(jnp.int32, (16, ATT_COLS), 1)
    is_gain = (lane >= GAIN_AT) & (lane < GAIN_AT + 2)
    att = att_own[...].reshape(16, ATT_COLS)
    gate_sum, down_sum = gate_own[...], down_own[...]
    squares = jnp.sum(jnp.where(is_gain, 0.0, att * att))
    squares = squares + jnp.sum(gate_sum * gate_sum) + jnp.sum(down_sum * down_sum)
    mine = slots_line.at[x, c]
    mine[0] = jnp.where(is_gain, att, 0.0)[:, LAST:]
    mine[1] = jnp.full((16, 128), 1.0, f32) * squares
    copies = [sems.copy(mine, mine, peer) for peer in line]
    for copy in copies:
        copy.start()
    for copy in copies:
        copy.wait()
    total = jnp.zeros((8, 128), f32)
    for i in range(RING):
        gain = slots_line[i, 0, 0] + slots_line[i, 1, 0]
        total = total + (slots_line[i, 0, 1, 0:8] + slots_line[i, 1, 1, 0:8]) + jnp.sum(gain * gain)
    mine = slots.at[y, z]
    mine[...] = total
    copies = [sems.copy(mine, mine, peer) for peer in plane]
    for copy in copies:
        copy.start()
    for copy in copies:
        copy.wait()
    total = slots[0, 0]
    for number in range(1, RING * RING):
        total = total + slots[number // RING, number % RING]
    norm_out[...] = jnp.sqrt(total)

    for copy in shares:
        copy.wait()
    gate_pieces = [gate_in[rank // 2, rank % 2] for rank in range(RANKS)]
    gate_out[...] = jnp.concatenate(
        [piece[:, :SLICE] for piece in gate_pieces]
        + [piece[:, HID : HID + SLICE] for piece in gate_pieces],
        axis=1,
    )
    att_pair[c] = att_own[c]
    pair.wait()
    one, two = att_pair[0], att_pair[1]
    k_at, v_at = LATE + HEAD_DIM, LATE + 2 * HEAD_DIM
    in_out[...] = jnp.concatenate(
        [
            one[:, :HEADS_6],
            one[:, LATE:k_at],
            two[:, :HEADS_6],
            two[:, LATE:k_at],
            one[:, k_at:v_at],
            two[:, k_at:v_at],
            one[:, v_at : v_at + HEAD_DIM],
            two[:, v_at : v_at + HEAD_DIM],
        ],
        axis=1,
    )
    out_out[...] = jnp.concatenate(
        [one[:, HEADS_6:LATE], one[:, LAST:GAIN_AT], two[:, HEADS_6:LATE], two[:, LAST:GAIN_AT]],
        axis=1,
    )
    gains_out[...] = one[:, LAST:] + two[:, LAST:]

    @pl.when(target != me)
    def _():
        move.wait()

    @pl.when(target == me)
    def _():
        stay.wait()


def settle(*args):
    scratch = [
        *(VM((RING, RING, RING, count, 2 * HEAD_DIM), bf16) for _, _, count in ROW_SPLITS),
        VM((CHIP, WIDE), bf16),
        VM((2, LOCAL, WIDE), bf16),
        VM((2, LOCAL, OUT_COLS), bf16),
        VM((2, LOCAL, WIDE), bf16),
        VM((WIDE, ATT_COLS), bf16),
        VM((RING, 2, LOCAL, WIDE), bf16),
        VM((RING, RING, DOWN_PAD, D), bf16),
        VM((16, RING, 16, 2 * HID), bf16),
        VM((WIDE, D), bf16),
        VM((CHIP, 2 * HEAD_DIM), f32),
        VM((2, LOCAL, WIDE), f32),
        VM((LOCAL, WIDE), f32),
        VM((2, 8, ATT_COLS), f32),
        VM((RING, 2, 8, 2 * HID), f32),
        VM((DOWN_PAD, D), f32),
        *(VM((RING, RING, RING, 16, lanes), bf16) for _, _, lanes in EARLY_SPLITS + LATE_SPLITS),
        VM((RING, LOCAL, WIDE), bf16),
        VM((RING, RING, LOCAL // RING, WIDE), bf16),
        VM((LOCAL, WIDE), f32),
        VM((2, 8, ATT_COLS), f32),
        VM((RING, 2, 8, 2 * HID), f32),
        VM((RING, 2, 2, 16, 128), f32),
        VM((RING, RING, 8, 128), f32),
    ]
    scratch += [
        VM((RING, 2, 16, D), bf16),
        VM((RING, 2, 16, D), bf16),
        VM((2, RING, 32, D), bf16),
        VM((2, RING, 32, D), bf16),
    ] * 2
    for order, _, count in ROW_SPLITS:
        scratch += reduce_scratch(order, (count, 2 * HEAD_DIM))
    for order, _, lanes in EARLY_SPLITS:
        scratch += reduce_scratch(order, (16, lanes))
    block = (RING, LOCAL // RING, WIDE)
    scratch += [VM(block, bf16) for _ in range(5)] + [VM(block, f32)]
    for order, _, count in DOWN_SPLITS:
        scratch += reduce_scratch(order, (count, D))
    for order, _, lanes in LATE_SPLITS:
        scratch += reduce_scratch(order, (16, lanes), ring=False)
    return remote_call(
        settle_kernel,
        [
            ((LOCAL, D), bf16, VM),
            ((LOCAL, D), bf16, VM),
            ((8, 1152), f32, VM),
            ((8, D), f32, VM),
            ((8, 128), f32, VM),
            ((8, 2 * FF), f32, VM),
            ((DOWN_PAD, D), f32, VM),
            ((8, 128), f32, VM),
        ],
        [ANY] * 3 + [VM] * 3 + [ANY] * 5 + [VM] * 2 + [ANY] * 3 + [VM] * 2 + [ANY] + [VM] * 2,
        scratch,
        240,
        3,
        *args,
    )


def adam_step(weight, gradient, moment, square, factor, step_rate):
    gradient = gradient * factor
    moment = beta_first * moment + (1.0 - beta_first) * gradient
    square = beta_second * square + (1.0 - beta_second) * gradient * gradient
    moment_hat = moment / (1.0 - beta_first**STEP)
    square_hat = square / (1.0 - beta_second**STEP)
    updated = weight - step_rate * (
        moment_hat / (jnp.sqrt(square_hat) + adam_eps) + decay_rate * weight
    )
    return (updated, moment, square, updated.astype(bf16))


RATES = (
    matrix_rate * D ** (-0.5),
    matrix_rate * 5 ** (-0.5),
    matrix_rate * D ** (-0.5),
    matrix_rate * FF ** (-0.5),
    gain_rate,
)


def optimize_kernel(norm_ref, in_sum, out_sum, gains_sum, gate_sum, down_sum, *refs):
    states, outs = refs[:17], refs[17:]
    factor = 1.0 / jnp.maximum(norm_ref[0:1, 0:1], 1.0)
    gain_lane = GAIN_AT - LAST
    gains = gains_sum[...][:, gain_lane : gain_lane + 8]
    gains = jnp.concatenate([gains, jnp.zeros((8, 120), f32)], axis=1)
    gains = jnp.concatenate([gains, jnp.zeros((120, 128), f32)], axis=0).T
    sums = (
        in_sum[0:7],
        out_sum[0:7],
        gate_sum[0:7],
        down_sum[0:DOWN_ROWS],
        gains[0:2, 0:7],
    )
    for number, gradient in enumerate(sums):
        weight, moment, square = (ref[...] for ref in states[3 * number : 3 * number + 3])
        news = adam_step(weight, gradient, moment, square, factor, RATES[number])
        for ref, new in zip(outs[4 * number : 4 * number + 4], news):
            ref[...] = new
    for ref, new in zip(outs[20:], states[15:]):
        ref[...] = new[...]
    outs[22][...] = norm_ref[0:1, 0:1]


def optimize(norm, sums, states, rows):
    shapes = []
    for number in range(5):
        shape = states[3 * number].shape
        shapes += [jax.ShapeDtypeStruct(shape, f32)] * 3 + [jax.ShapeDtypeStruct(shape, bf16)]
    shapes += [jax.ShapeDtypeStruct((LOCAL, D), bf16)] * 2 + [jax.ShapeDtypeStruct((1, 1), f32)]
    return pl.pallas_call(
        optimize_kernel,
        out_shape=shapes,
        in_specs=[pl.BlockSpec(memory_space=VM)] * (6 + 17),
        out_specs=[pl.BlockSpec(memory_space=VM)] * 23,
        compiler_params=pltpu.CompilerParams(vmem_limit_bytes=56 << 20),
    )(norm, *sums, *states, *rows)


def rotation_table(doc_place):
    half_dim = HEAD_DIM // 2
    inverse = rope_base ** (-(jnp.arange(half_dim, dtype=f32) * 2.0) / HEAD_DIM)
    angles = doc_place.astype(f32)[:, None] * inverse[None, :]
    cosine, sine = jnp.cos(angles), jnp.sin(angles)
    return jnp.concatenate([cosine] * 4, axis=1), jnp.concatenate([-sine, sine] * 2, axis=1)


def body(
    tokens,
    cotangent,
    lengths,
    in_weight,
    out_weight,
    gate_weight,
    down_weight,
    gains,
    in_first,
    out_first,
    gate_first,
    down_first,
    gains_first,
    in_second,
    out_second,
    gate_second,
    down_second,
    gains_second,
):
    chip = (lax.axis_index("y") * RING + lax.axis_index("z")) * RING + lax.axis_index("x")
    widen, pack, turn, swap = widen_matrix(), pack_matrix(), turn_matrix(), swap_matrix()
    pair, gate_line, down_here, x_line, up_line = spread(
        tokens,
        cotangent,
        in_weight,
        out_weight.T,
        gains,
        gate_weight,
        down_weight,
        turn,
    )
    gate_all = lax.all_gather(gate_line, ("y", "z"), axis=0, tiled=False).reshape(WIDE, 2 * HID)
    down_all = lax.all_gather(down_here, ("y", "z"), axis=0, tiled=False).reshape(16 * DOWN_PAD, D)

    row = jnp.arange(CHIP, dtype=jnp.int32)
    position = (row % LOCAL) * DEVICES + 2 * chip + row // LOCAL
    starts = (jnp.cumsum(lengths) - lengths).astype(jnp.int32)
    begin = jnp.max(jnp.where(position[:, None] >= starts, starts, 0), axis=1)
    cosine, sine = rotation_table(position - begin)
    chip_place = (2 * chip).astype(jnp.int32).reshape(1)

    queries, normed, x_wide, gain_rows, att_all, *keys, up_line = project(
        x_line, up_line, pair, turn, swap, widen, order_matrix(), cosine, sine
    )
    att_flat = att_all.reshape(WIDE, ATT_COLS)
    mixed, mixed_wide, lse, keys, turned = attend(starts, chip_place, queries, *keys)
    middle, delta_middle, branch, gain_two, parts, grad_gate, grad_down = feed(
        mixed, att_flat, x_wide, gain_rows, gate_all, down_all, up_line, widen, pack
    )
    spread_over = dict(split_axis=0, concat_axis=0, tiled=True)
    grad_gate = grad_gate.reshape(16, RING, 16, 2 * HID)
    grad_gate = lax.all_to_all(grad_gate, ("y", "z"), **spread_over)
    delta_q, *delta_kv = attend_back(
        starts, chip_place, queries, branch, att_flat, keys, turned, mixed_wide, lse
    )
    output, input_grad, *sums, norm = settle(
        *delta_kv,
        delta_q,
        cosine,
        sine,
        normed,
        x_wide,
        mixed,
        branch,
        att_flat,
        gain_rows,
        gain_two,
        grad_gate,
        grad_down.reshape(RING, RING, DOWN_PAD, D),
        parts,
        middle,
        delta_middle,
        widen_matrix(turned=True),
        turn,
        swap,
    )

    states = (
        *(in_weight, in_first, in_second),
        *(out_weight.T, out_first.T, out_second.T),
        *(gate_weight, gate_first, gate_second),
        *(down_weight, down_first, down_second),
        *(gains, gains_first, gains_second),
    )
    new = optimize(norm, sums, states, (output, input_grad))
    out_new = [values.T for values in new[4:8]]
    return (*new[20:22], *new[:4], *out_new, *new[8:20], new[22].reshape(()))


def solution(mesh):
    grid = Mesh(mesh.devices.reshape(RING, RING, RING, 2), ALL)
    rows, columns = P(ALL, None), P(None, ALL)
    return jax.shard_map(
        body,
        mesh=grid,
        in_specs=(
            rows,
            rows,
            P(),
            rows,
            columns,
            rows,
            rows,
            columns,
            rows,
            columns,
            rows,
            rows,
            columns,
            rows,
            columns,
            rows,
            rows,
            columns,
        ),
        out_specs=(
            rows,
            rows,
            *[rows] * 4,
            *[columns] * 4,
            *[rows] * 8,
            *[columns] * 4,
            P(),
        ),
        check_vma=False,
    )
```
